32 devices in a mesh: dp: 16 (over z, x, core), blk: 2 (over y).
Axes of the slice: x: 2, y: 2, z: 4, core: 2. Of those that a mesh axis runs over, the one named last changes fastest.
Arguments:
- attn_cols: bfloat16 [4096, 7168], P('blk', 'dp'), may hold values from -6 to 6
- residual: bfloat16 [4096, 7168], P(('blk', 'dp')), may hold values from -80 to 80
- norm_gain: bfloat16 [7168], replicated, may hold values from 0.5 to 1.5
- router_weight: bfloat16 [7168, 16], replicated, may hold values from -0.0625 to 0.0625
- expert_ids: int32 [4096, 2], P(('blk', 'dp')), may hold values from 0 to 15, all different within a row; in each aligned block of 128 rows (0 to 127, 128 to 255, ...) at most 20 rows name the same one
- gate_weight: bfloat16 [16, 7168, 1024], P('dp', None, 'blk'), may hold values from -0.0625 to 0.0625
- up_weight: bfloat16 [16, 7168, 1024], P('dp', None, 'blk'), may hold values from -0.0625 to 0.0625
- down_weight: bfloat16 [16, 7168, 1024], P('dp', 'blk'), may hold values from -0.1875 to 0.1875
Outputs:
- layer_out: bfloat16 [4096, 7168], P(('blk', 'dp'))
The draws below stay inside these ranges and needn't reach their ends.
Inputs may be any that keep to these rules, and one draw needn't show every extreme that they name: `expert_ids`: within each aligned block of 128 rows (the rows of one device) no expert is named by more than 20 rows, and in some block some expert is named by exactly 20 rows; the 2 experts of a row differ.
All inputs are finite; a program needn't handle non-finite values.
Results may differ from the reference program's by a relative error of at most 0.0044.
Values may be sent and summed in bfloat16 or wider, within the bound.
No kernel may reach another device: no remote copies, remote signals or barrier semaphores. Data moves between devices by JAX's collectives and lax.ppermute only.
A program may use at most 192 MiB of HBM per device.

```python
import math
import jax
import jax.numpy as jnp
import numpy as np
from jax import lax

D = 7168
FF = 1024
TOP = 2
TOK_DEV = 128
EXPERTS = 16
CAP = 20
TOKENS = 4096


def draw_residual(key, part):
    key = jax.random.fold_in(key, 7)
    first, second, third = jax.random.split(key, 3)
    rowscale = jnp.exp(jax.random.uniform(first, (TOKENS, 1)) * math.log(10.0)) / math.sqrt(10.0)
    base = jnp.clip(jax.random.normal(third, (TOKENS, D)), -4.0, 4.0)
    colscale = jnp.exp(jax.random.uniform(second, (1, D)) * math.log(10.0)) / math.sqrt(10.0)
    return (base * rowscale * colscale).astype(jnp.bfloat16)


def level_of(own_key, extent, cuts, least, largest):
    def one(dim, parts):
        heights = jax.random.uniform(jax.random.fold_in(jax.random.fold_in(own_key, 6), dim), (parts,), jnp.float32, least / len(cuts), largest / len(cuts))
        return jnp.repeat(jnp.exp(heights), extent[dim] // parts).reshape((-1,) + (1,) * (len(extent) - dim - 1))

    level = one(*cuts[0])
    for cut in cuts[1:]:
        level = level * one(*cut)
    return level


def assign_block(own_key, own, number, rows, amount, top, limit, lean):
    order = jax.random.permutation(own_key, amount)
    packed, common = load_shares(amount, rows * top, limit, lean, True), load_shares(amount, rows * top, limit, lean, False)
    places = jnp.arange(amount)

    def named(sizes, turn):
        used = int((sizes > 0).sum())
        fixed = max(1, used // 4)
        shifted = fixed + (places - fixed + turn * (used - fixed)) % max(1, amount - fixed)
        return jnp.zeros((amount,), jnp.int32).at[order[jnp.where(places < fixed, places, shifted)]].set(jnp.asarray(sizes, jnp.int32))

    sizes = jnp.where(number % 4 == 0, named(packed, number // 4), named(common, number - number // 4 - 1))
    mixed = jax.random.permutation(jax.random.fold_in(own, 3), amount)
    donor, taker = mixed[0:amount // 2 * 2:2], mixed[1:amount // 2 * 2:2]
    margin = jnp.minimum(sizes[donor] - 1, limit - sizes[taker]) // 2
    margin = jnp.where((donor == order[0]) | (taker == order[0]) | (sizes[taker] == 0), 0, jnp.maximum(margin, 0))
    shifted = jax.random.randint(jax.random.fold_in(own, 4), (amount // 2,), 0, 1 << 20) % (margin + 1)
    sizes = sizes.at[donor].add(-shifted).at[taker].add(shifted)
    members = jnp.searchsorted(jnp.cumsum(sizes), jnp.arange(rows * top), side="right").astype(jnp.int32)
    listing = members.reshape(top, rows).T
    listing = listing[jax.random.permutation(jax.random.fold_in(own, 1), rows)]
    turn = jax.random.randint(jax.random.fold_in(own, 2), (rows, 1), 0, top)
    return jnp.take_along_axis(listing, (jnp.arange(top)[None, :] + turn) % top, axis=1)


def load_shares(count, total, bound, skew, full):
    loads = [(1 << 20) // math.isqrt(standing ** skew) + 1 for standing in range(1, count + 1)]
    largest = bound if full else min(bound, max(-(-total // count), total * loads[0] // sum(loads)))
    least = 1 if total - largest >= count - 1 else 0
    counts, spare = [largest] + [least] * (count - 1), total - largest - least * (count - 1)
    while spare > 0:
        candidates = [i for i in range(1, count) if counts[i] < largest] or [i for i in range(1, count) if counts[i] < bound]
        pool, remaining = sum([loads[i] for i in candidates]), spare
        for i in candidates:
            more = min(bound - counts[i], max(1, remaining * loads[i] // pool), spare)
            counts[i] = counts[i] + more
            spare = spare - more
    return np.array(counts)


def noise(own_key, extent, scale, bound, pieces=(), held_as=jnp.bfloat16):
    array = scale * jax.random.normal(own_key, extent, jnp.float32)
    if pieces:
        array = array * level_of(own_key, extent, pieces, -0.22, 0.18)
    return jnp.clip(array, -bound, bound).astype(held_as)


def setup_inputs(seed: int = 0) -> dict:
    arg_keys = jax.random.split(jax.random.key(seed), 9)
    attn_cols = noise(arg_keys[0], (TOKENS, D), 1.0, 6.0, ((0, 2), (1, 16)))
    residual = draw_residual(jax.random.fold_in(arg_keys[8], 71), 0)
    norm_gain = jnp.clip(1.0 + 0.1 * jax.random.normal(arg_keys[2], (D,), jnp.float32), 0.5, 1.5).astype(jnp.bfloat16)
    router_weight = noise(arg_keys[3], (D, EXPERTS), D ** -0.5, 0.0625)
    expert_ids_keys = jax.random.split(jax.random.fold_in(arg_keys[4], 1), TOKENS // TOK_DEV)
    expert_ids_turns = jax.random.permutation(jax.random.fold_in(arg_keys[4], 3), TOKENS // TOK_DEV)
    expert_ids = jax.vmap(lambda own, number: assign_block(jax.random.fold_in(arg_keys[4], 2), own, number, TOK_DEV, EXPERTS, TOP, CAP, 1))(expert_ids_keys, expert_ids_turns).reshape((TOKENS, TOP))
    gate_weight = noise(arg_keys[5], (EXPERTS, D, FF), D ** -0.5, 0.0625, ((0, 16), (2, 2)))
    up_weight = noise(arg_keys[6], (EXPERTS, D, FF), D ** -0.5, 0.0625, ((0, 16), (2, 2)))
    down_weight = noise(arg_keys[7], (EXPERTS, D, FF), FF ** -0.5, 0.1875, ((0, 16), (1, 2)))
    return {"attn_cols": attn_cols, "residual": residual, "norm_gain": norm_gain, "router_weight": router_weight, "expert_ids": expert_ids, "gate_weight": gate_weight, "up_weight": up_weight, "down_weight": down_weight}


def expert_ffn(rows, gate_one, up_one, down_one):
    gated = jnp.dot(rows, gate_one, preferred_element_type=jnp.float32)
    upward = jnp.dot(rows, up_one, preferred_element_type=jnp.float32)
    hidden = (jax.nn.silu(gated) * upward).astype(jnp.bfloat16)
    return jnp.dot(hidden, down_one.T, preferred_element_type=jnp.float32).astype(jnp.bfloat16)

def reference(attn_cols, residual, norm_gain, router_weight, expert_ids, gate_weight, up_weight, down_weight):
    stream = residual.astype(jnp.float32) + attn_cols.astype(jnp.float32)
    meansq = lax.optimization_barrier(jnp.mean(stream * stream, axis=1, keepdims=True))
    normed = (stream * lax.rsqrt(meansq + 1e-06) * norm_gain.astype(jnp.float32)).astype(jnp.bfloat16)
    affinity = jax.nn.sigmoid(jnp.dot(normed, router_weight, preferred_element_type=jnp.float32))
    chosen = jnp.take_along_axis(affinity, expert_ids, axis=1)
    weights = 2.5 * chosen / lax.optimization_barrier(jnp.sum(chosen, axis=1, keepdims=True))
    devices = TOKENS // TOK_DEV
    flat_ids = expert_ids.reshape(devices, TOK_DEV * TOP)
    onehot = (flat_ids[:, :, None] == jnp.arange(EXPERTS, dtype=jnp.int32)[None, None, :]).astype(jnp.int32)
    before = jnp.cumsum(onehot, axis=1) - onehot
    ranks = lax.optimization_barrier(jnp.sum(before * onehot, axis=2)).astype(jnp.int32)
    slots = (flat_ids * CAP + ranks).astype(jnp.int32)
    dev_index = jnp.arange(devices, dtype=jnp.int32)[:, None]
    owner_tok = (dev_index * TOK_DEV + jnp.arange(TOK_DEV * TOP, dtype=jnp.int32)[None, :] // TOP).astype(jnp.int32)
    table = jnp.full((devices, EXPERTS * CAP), TOKENS, dtype=jnp.int32)
    table = table.at[jnp.broadcast_to(dev_index, slots.shape), slots].set(owner_tok)
    table = table.reshape(devices, EXPERTS, CAP).transpose(1, 0, 2).reshape(EXPERTS, devices * CAP)
    padded = jnp.concatenate([normed, jnp.zeros((1, D), normed.dtype)], axis=0)

    def one_expert(inputs):
        row_index, gate_one, up_one, down_one = inputs
        return expert_ffn(padded[row_index], gate_one, up_one, down_one)
    outputs = lax.map(one_expert, (table, gate_weight, up_weight, down_weight))
    row_pos = (dev_index * CAP + ranks).astype(jnp.int32)
    picked = outputs[flat_ids, row_pos].reshape(TOKENS, TOP, D)
    summed = stream
    for member in range(TOP):
        summed = summed + weights[:, member:member + 1] * picked[:, member].astype(jnp.float32)
    return summed.astype(jnp.bfloat16)
```

```python
import functools

import jax
import jax.numpy as jnp
from jax import lax
from jax.experimental import pallas as pl
from jax.experimental.pallas import tpu as pltpu
from jax.sharding import PartitionSpec as P

FOLD = 4
TURNS = 2
VMEM = 48 * 1024 * 1024
F32 = jnp.float32
BF16 = jnp.bfloat16


def dot(a, b):
    return lax.dot_general(a, b, (((1,), (0,)), ((), ())), preferred_element_type=F32)


def dot_nt(a, b):
    return lax.dot_general(a, b, (((1,), (1,)), ((), ())), preferred_element_type=F32)


def as_mask(cond):
    return jnp.where(cond, 1.0, 0.0).astype(BF16)


def pack_turn(base, turn, aux_ref, normed, slabs):
    tokens, width = normed.shape
    quarter = width // FOLD
    more = base // FOLD
    rows = len(slabs) * base
    row = lax.broadcasted_iota(jnp.int32, (rows, tokens), 0).astype(F32)
    at = 2 + 4 * turn
    whole = as_mask((row == aux_ref[at : at + 1, :]) | (row == aux_ref[at + 1 : at + 2, :]))
    folded = jnp.zeros((rows, quarter), F32)
    for k in range(FOLD):
        cols = slice(k * quarter, (k + 1) * quarter)
        block = dot(whole, normed[:, cols]).astype(BF16)
        for p, slab in enumerate(slabs):
            slab[:, cols] = block[p * base : (p + 1) * base]
        shift = row - k * more
        rest = (shift == aux_ref[at + 2 : at + 3, :]) | (shift == aux_ref[at + 3 : at + 4, :])
        folded += dot(as_mask(rest), normed[:, cols])
    folded = folded.astype(BF16)
    for p, slab in enumerate(slabs):
        slab[:, width:] = folded[p * base : (p + 1) * base]


def first_kernel(base, me_ref, attn_ref, res_ref, gain_ref, router_ref, ids_ref, aux_ref, normed_ref, *refs):
    slabs, held = refs[:-1], refs[-1]
    tokens, width = res_ref.shape
    experts = router_ref.shape[0]
    quarter = width // FOLD
    total = jnp.zeros((tokens, 1), F32)
    for k in range(FOLD):
        cols = slice(k * quarter, (k + 1) * quarter)
        part = res_ref[:, cols].astype(F32) + attn_ref[cols, :].astype(F32).T
        held[:, cols] = part
        total += jnp.sum(part * part, axis=1, keepdims=True)
    scale = lax.rsqrt(total / width + 1e-06)
    logits = jnp.zeros((experts, tokens), F32)
    for k in range(FOLD):
        cols = slice(k * quarter, (k + 1) * quarter)
        piece = (held[:, cols] * scale * gain_ref[:, cols].astype(F32)).astype(BF16)
        normed_ref[:, cols] = piece
        logits += dot_nt(router_ref[:, cols], piece)
    affinity = jax.nn.sigmoid(logits)
    expert = lax.broadcasted_iota(jnp.int32, (experts, tokens), 0)
    hit = [expert == ids_ref[k : k + 1, :] for k in range(2)]
    named = as_mask(hit[0] | hit[1])
    first = lax.broadcasted_iota(jnp.int32, (tokens, tokens), 0)
    second = lax.broadcasted_iota(jnp.int32, (tokens, tokens), 1)
    before = dot(named, as_mask(first < second))
    chosen = [jnp.sum(jnp.where(h, affinity, 0.0), axis=0, keepdims=True) for h in hit]
    ranks = [
        jnp.sum(jnp.where(h, before, 0.0), axis=0, keepdims=True).astype(jnp.int32) for h in hit
    ]
    denom = chosen[0] + chosen[1]
    aux_ref[...] = jnp.zeros_like(aux_ref)
    for k in range(2):
        aux_ref[k : k + 1, :] = 2.5 * chosen[k] / denom
        offset = ids_ref[k : k + 1, :] - me_ref[0]
        offset = jnp.where(offset < 0, offset + experts, offset)
        for turn in range(TURNS):
            here = offset % TURNS == turn
            row = offset // TURNS * base + ranks[k]
            at = 2 + 4 * turn + k
            main = jnp.where(here & (ranks[k] < base), row, -experts * base)
            rest = jnp.where(here & (ranks[k] >= base), row - base, -experts * base)
            aux_ref[at : at + 1, :] = main.astype(F32)
            aux_ref[at + 2 : at + 3, :] = rest.astype(F32)
    pack_turn(base, 0, aux_ref, normed_ref, slabs)


def first(base, me, attn, residual, gain, router, ids):
    tokens, width = residual.shape
    count = router.shape[0] // TURNS
    slab = jax.ShapeDtypeStruct((base, width + width // FOLD), BF16)
    return pl.pallas_call(
        functools.partial(first_kernel, base),
        in_specs=[pl.BlockSpec(memory_space=pltpu.SMEM)] + [pl.BlockSpec(memory_space=pltpu.VMEM)] * 5,
        out_shape=[
            jax.ShapeDtypeStruct((16, tokens), F32),
            jax.ShapeDtypeStruct((tokens, width), BF16),
        ]
        + [slab] * count,
        scratch_shapes=[pltpu.VMEM((tokens, width), F32)],
        compiler_params=pltpu.CompilerParams(vmem_limit_bytes=VMEM),
        cost_estimate=pl.CostEstimate(
            flops=2 * count * base * tokens * width,
            bytes_accessed=10 * tokens * width,
            transcendentals=0,
        ),
        name="first",
    )(me, attn, residual, gain, router, ids)


def others_kernel(base, turn, attn_ref, res_ref, aux_ref, normed_ref, stream_ref, *slabs):
    pack_turn(base, turn, aux_ref, normed_ref, slabs)
    width = res_ref.shape[1]
    quarter = width // FOLD
    for k in range(FOLD):
        cols = slice(k * quarter, (k + 1) * quarter)
        stream_ref[:, cols] = res_ref[:, cols].astype(F32) + attn_ref[cols, :].astype(F32).T


def others(base, turn, attn, residual, aux, normed, count):
    tokens, width = residual.shape
    slab = jax.ShapeDtypeStruct((base, width + width // FOLD), BF16)
    return pl.pallas_call(
        functools.partial(others_kernel, base, turn),
        out_shape=[jax.ShapeDtypeStruct((tokens, width), F32)] + [slab] * count,
        compiler_params=pltpu.CompilerParams(vmem_limit_bytes=VMEM),
        cost_estimate=pl.CostEstimate(
            flops=2 * count * base * tokens * width,
            bytes_accessed=12 * tokens * width,
            transcendentals=0,
        ),
        name="others",
    )(attn, residual, aux, normed)


def inward_kernel(base, *refs):
    slabs, (gate_ref, up_ref, out_ref, acc) = refs[:-4], refs[-4:]
    quarter, ff = gate_ref.shape[1:]
    more = base // FOLD
    rows = len(slabs) * base
    few = len(slabs) * more
    step = pl.program_id(0)

    @pl.when(step == 0)
    def _():
        acc[...] = jnp.zeros_like(acc)

    cols = pl.ds(pl.multiple_of(step * quarter, quarter), quarter)
    behind = jnp.concatenate([slab[:, quarter * FOLD :] for slab in slabs], axis=0)
    out_row = lax.broadcasted_iota(jnp.int32, (few, rows), 0)
    in_row = lax.broadcasted_iota(jnp.int32, (few, rows), 1)
    select = as_mask(in_row == (out_row // more) * base + step * more + out_row % more)
    rest = dot(select, behind).astype(BF16)
    block = jnp.concatenate([slab[:, cols] for slab in slabs] + [rest], axis=0)
    acc[:, :ff] += dot(block, gate_ref[0])
    acc[:, ff:] += dot(block, up_ref[0])

    @pl.when(step == FOLD - 1)
    def _():
        gated = acc[:, :ff]
        out_ref[...] = (gated / (1.0 + jnp.exp(-gated)) * acc[:, ff:]).astype(BF16)


def inward(base, slabs, gate, up):
    width, ff = gate.shape[1:]
    quarter = width // FOLD
    total = len(slabs) * (base + base // FOLD)
    return pl.pallas_call(
        functools.partial(inward_kernel, base),
        grid=(FOLD,),
        in_specs=[pl.BlockSpec(slabs[0].shape, lambda i: (0, 0))] * len(slabs)
        + [pl.BlockSpec((1, quarter, ff), lambda i: (0, i, 0))] * 2,
        out_specs=pl.BlockSpec((total, ff), lambda i: (0, 0)),
        out_shape=jax.ShapeDtypeStruct((total, ff), BF16),
        scratch_shapes=[pltpu.VMEM((total, 2 * ff), F32)],
        compiler_params=pltpu.CompilerParams(vmem_limit_bytes=VMEM),
        cost_estimate=pl.CostEstimate(flops=total, bytes_accessed=total, transcendentals=0),
        name="inward",
    )(*slabs, gate, up)


def outward_kernel(base, fold, parts, here_ref, *refs):
    hidden, down_ref, slabs, folded = refs[:parts], refs[parts], refs[parts + 1 : -1], refs[-1]
    step = pl.program_id(0)
    here = here_ref[0]
    more = base // FOLD
    rows = len(slabs) * base
    few = len(slabs) * more
    ff = hidden[0].shape[1]

    @pl.when(step == 0)
    def _():
        folded[...] = jnp.zeros_like(folded)

    @pl.when(step < fold)
    def _():
        made = None
        for o in range(parts):
            order = [(j - o) % parts for j in range(parts)]
            main, rest = rows // parts, few // parts
            block = jnp.concatenate(
                [hidden[o][i * main : (i + 1) * main, :] for i in order]
                + [hidden[o][rows + i * rest : rows + (i + 1) * rest, :] for i in order],
                axis=0,
            )
            at = pl.multiple_of(lax.rem(here + parts - o, parts) * ff, ff)
            term = dot_nt(block, down_ref[0, :, pl.ds(at, ff)])
            made = term if made is None else made + term
        made = made.astype(BF16)
        out_row = lax.broadcasted_iota(jnp.int32, (rows, few), 0)
        in_row = lax.broadcasted_iota(jnp.int32, (rows, few), 1)
        place = as_mask(out_row == (in_row // more) * base + step * more + in_row % more)
        for p, slab in enumerate(slabs):
            slab[...] = made[p * base : (p + 1) * base]
        folded[...] += dot(place, made[rows:])

    @pl.when(step == fold)
    def _():
        last = folded[...].astype(BF16)
        for p, slab in enumerate(slabs):
            slab[...] = last[p * base : (p + 1) * base]


def outward(base, fold, count, here, hidden, down):
    parts = len(hidden)
    total, ff = hidden[0].shape
    cols = down.shape[1]
    step = cols // fold
    return pl.pallas_call(
        functools.partial(outward_kernel, base, fold, parts),
        grid_spec=pltpu.PrefetchScalarGridSpec(
            num_scalar_prefetch=1,
            grid=(fold + 1,),
            in_specs=[pl.BlockSpec((total, ff), lambda i, here: (0, 0))] * parts
            + [pl.BlockSpec((1, step, parts * ff), lambda i, here: (0, jnp.minimum(i, fold - 1), 0))],
            out_specs=[pl.BlockSpec((base, step), lambda i, here: (0, i))] * count,
            scratch_shapes=[pltpu.VMEM((count * base, step), F32)],
        ),
        out_shape=[jax.ShapeDtypeStruct((base, cols + step), BF16)] * count,
        compiler_params=pltpu.CompilerParams(vmem_limit_bytes=VMEM),
        cost_estimate=pl.CostEstimate(flops=total, bytes_accessed=total, transcendentals=0),
        name="outward",
    )(here, *hidden, down)


def combine_kernel(base, fold, turn, parts, here_ref, aux_ref, stream_ref, *refs):
    slabs, out_ref = refs[:-1], refs[-1]
    count = len(slabs) // parts
    tokens = out_ref.shape[0]
    cols = out_ref.shape[1] // parts
    step = cols // fold
    more = base // FOLD
    row = lax.broadcasted_iota(jnp.int32, (count * base, tokens), 0).astype(F32)
    at = 2 + 4 * turn

    def matrix(start, shift):
        both = jnp.where(row - shift == aux_ref[start : start + 1, :], aux_ref[0:1, :], 0.0)
        both += jnp.where(row - shift == aux_ref[start + 1 : start + 2, :], aux_ref[1:2, :], 0.0)
        both = both.T
        high = both.astype(BF16)
        return high, (both - high.astype(F32)).astype(BF16)

    high, low = matrix(at, 0)
    rests = [matrix(at + 2, q * more) for q in range(fold)]
    for o in range(parts):
        start = lax.rem(here_ref[0] + o, parts) * cols
        back = jnp.concatenate([slab[...] for slab in slabs[o * count : (o + 1) * count]], axis=0)
        for q, (rest_high, rest_low) in enumerate(rests):
            main = back[:, q * step : (q + 1) * step]
            behind = back[:, cols:]
            total = dot(low, main) + dot(rest_low, behind)
            total += dot(high, main) + dot(rest_high, behind)
            cut = pl.ds(pl.multiple_of(start + q * step, step), step)
            out_ref[:, cut] = (stream_ref[:, cut] + total).astype(out_ref.dtype)


def combine(base, fold, turn, parts, here, aux, stream, slabs):
    tokens, width = stream.shape
    last = turn == TURNS - 1
    return pl.pallas_call(
        functools.partial(combine_kernel, base, fold, turn, parts),
        in_specs=[pl.BlockSpec(memory_space=pltpu.SMEM)]
        + [pl.BlockSpec(memory_space=pltpu.VMEM)] * (2 + len(slabs)),
        out_shape=jax.ShapeDtypeStruct((tokens, width), BF16 if last else F32),
        compiler_params=pltpu.CompilerParams(vmem_limit_bytes=VMEM),
        cost_estimate=pl.CostEstimate(
            flops=4 * tokens * width * len(slabs) // parts * base,
            bytes_accessed=8 * tokens * width,
            transcendentals=0,
        ),
        name="combine",
    )(here, aux, stream, *slabs)


def body(
    attn_cols, residual, norm_gain, router_weight, expert_ids, gate_weight, up_weight, down_weight
):
    groups = lax.axis_size("dp")
    parts = lax.axis_size("blk")
    tokens, width = residual.shape
    experts = router_weight.shape[1]
    fanout = expert_ids.shape[1]
    assert gate_weight.shape[0] == 1 and fanout == 2 and groups % TURNS == 0
    capacity = max(2, (5 * tokens * fanout + 4 * experts - 1) // (4 * experts))
    base = capacity * FOLD // (FOLD + 1)
    assert base * (FOLD + 1) == capacity * FOLD and base % FOLD == 0
    cols = down_weight.shape[1]
    fold = max(f for f in (1, 2, FOLD) if cols % (128 * f) == 0)
    count = groups // TURNS
    me = lax.axis_index("dp").astype(jnp.int32).reshape(1)
    here = lax.axis_index("blk").astype(jnp.int32).reshape(1)

    def across(block, shift):
        perm = [(i, (i + shift) % parts) for i in range(parts)]
        return lax.ppermute(block, "blk", perm) if shift else block

    def forth(slab, offset):
        perm = [(i, (i + offset) % groups) for i in range(groups)]
        return lax.ppermute(slab, "dp", perm) if offset else slab

    def back(slab, offset, shift):
        perm = [
            (i * parts + j, (i - offset) % groups * parts + (j - shift) % parts)
            for i in range(groups)
            for j in range(parts)
        ]
        return lax.ppermute(slab, ("dp", "blk"), perm) if offset or shift else slab

    held = attn_cols.shape[1]
    send = attn_cols.T.reshape(held, groups, tokens).transpose(1, 0, 2)
    attn = lax.all_to_all(send, "dp", split_axis=0, concat_axis=0, tiled=True)
    attn = attn.reshape(width, tokens)
    aux, normed, *slabs = first(
        base, me, attn, residual, norm_gain.reshape(1, width), router_weight.T, expert_ids.T
    )
    stream, *rest = others(base, 1, attn, residual, aux, normed, count)
    arrived = []
    for turn, packs in enumerate((slabs, rest)):
        own = [None] * count
        for p in sorted(range(count), key=lambda p: abs(TURNS * p + turn - groups // 2)):
            own[p] = forth(packs[p], TURNS * p + turn)
        arrived.append([across(slab, o) for o in range(parts) for slab in own])
    returned = None
    for turn in range(TURNS):
        if returned is not None:
            half = len(returned) // 2
            arrived[turn], returned[:half] = lax.optimization_barrier(
                (arrived[turn], returned[:half])
            )
        hidden = inward(base, arrived[turn], gate_weight, up_weight)
        hidden = [across(hidden, o) for o in range(parts)]
        made = outward(base, fold, count * parts, here, hidden, down_weight)
        returned = [
            back(made[o * count + p], TURNS * p + turn, o)
            for o in range(parts)
            for p in range(count)
        ]
        if turn == 0:
            ready = returned
    stream = combine(base, fold, 0, parts, here, aux, stream, ready)
    return combine(base, fold, 1, parts, here, aux, stream, returned)


def solution(mesh):
    return jax.shard_map(
        body,
        mesh=mesh,
        in_specs=(
            P("blk", "dp"),
            P(("blk", "dp"), None),
            P(),
            P(),
            P(("blk", "dp"), None),
            P("dp", None, "blk"),
            P("dp", None, "blk"),
            P("dp", "blk", None),
        ),
        out_specs=P(("blk", "dp"), None),
        check_vma=False,
    )
```

```python
import functools

import jax
import jax.numpy as jnp
from jax import lax
from jax.experimental import pallas as pl
from jax.experimental.pallas import tpu as pltpu
from jax.sharding import PartitionSpec as P

FOLDS = (1, 1, 2)
STEPS = 4
VMEM = 58 * 1024 * 1024
F32 = jnp.float32
BF16 = jnp.bfloat16


def dot(a, b):
    return lax.dot_general(a, b, (((1,), (0,)), ((), ())), preferred_element_type=F32)


def dot_nt(a, b):
    return lax.dot_general(a, b, (((1,), (1,)), ((), ())), preferred_element_type=F32)


def as_mask(cond):
    return jnp.where(cond, 1.0, 0.0).astype(BF16)


def placed(aux_ref, group, rows, shift):
    row = lax.broadcasted_iota(jnp.int32, (rows, aux_ref.shape[1]), 0).astype(F32) - shift
    at = 2 + 2 * group
    return [row == aux_ref[at + k : at + k + 1, :] for k in range(2)]


def pack_group(base, group, aux_ref, normed, pack_ref):
    fold = FOLDS[group]
    cols = pack_ref.shape[1]
    block = min(cols, normed.shape[1] // STEPS)
    picks = []
    for h in range(fold):
        first, second = placed(aux_ref, group, pack_ref.shape[0], h * (base // fold))
        picks.append(as_mask(first | second))
    for c in range(0, cols, block):
        total = None
        for h in range(fold):
            term = dot(picks[h], normed[:, h * cols + c : h * cols + c + block])
            total = term if total is None else total + term
        pack_ref[:, c : c + block] = total.astype(BF16)


def first_kernel(base, attn_ref, res_ref, gain_ref, router_ref, ids_ref, aux_ref, normed_ref, pack_ref, held):
    tokens, width = res_ref.shape
    experts = router_ref.shape[0]
    quarter = width // STEPS
    total = jnp.zeros((tokens, 1), F32)
    for k in range(STEPS):
        cols = slice(k * quarter, (k + 1) * quarter)
        part = res_ref[:, cols].astype(F32) + attn_ref[cols, :].astype(F32).T
        held[:, cols] = part
        total += jnp.sum(part * part, axis=1, keepdims=True)
    scale = lax.rsqrt(total / width + 1e-06)
    logits = jnp.zeros((experts, tokens), F32)
    for k in range(STEPS):
        cols = slice(k * quarter, (k + 1) * quarter)
        piece = (held[:, cols] * scale * gain_ref[:, cols].astype(F32)).astype(BF16)
        normed_ref[:, cols] = piece
        logits += dot_nt(router_ref[:, cols], piece)
    affinity = jax.nn.sigmoid(logits)
    expert = lax.broadcasted_iota(jnp.int32, (experts, tokens), 0)
    hit = [expert == ids_ref[k : k + 1, :] for k in range(2)]
    named = as_mask(hit[0] | hit[1])
    first = lax.broadcasted_iota(jnp.int32, (tokens, tokens), 0)
    second = lax.broadcasted_iota(jnp.int32, (tokens, tokens), 1)
    before = dot(named, as_mask(first < second))
    chosen = [jnp.sum(jnp.where(h, affinity, 0.0), axis=0, keepdims=True) for h in hit]
    ranks = [
        jnp.sum(jnp.where(h, before, 0.0), axis=0, keepdims=True).astype(jnp.int32) for h in hit
    ]
    denom = chosen[0] + chosen[1]
    for k in range(2):
        aux_ref[k : k + 1, :] = 2.5 * chosen[k] / denom
        start = 0
        for g, fold in enumerate(FOLDS):
            slots = base // fold
            inside = (ranks[k] >= start) & (ranks[k] < start + slots)
            row = ids_ref[k : k + 1, :] * base + ranks[k] - start
            at = 2 + 2 * g + k
            aux_ref[at : at + 1, :] = jnp.where(inside, row, -experts * base).astype(F32)
            start += slots
    pack_group(base, 0, aux_ref, normed_ref, pack_ref)


def first(base, attn, residual, gain, router, ids):
    tokens, width = residual.shape
    rows = router.shape[0] * base
    return pl.pallas_call(
        functools.partial(first_kernel, base),
        out_shape=[
            jax.ShapeDtypeStruct((8, tokens), F32),
            jax.ShapeDtypeStruct((tokens, width), BF16),
            jax.ShapeDtypeStruct((rows, width // FOLDS[0]), BF16),
        ],
        scratch_shapes=[pltpu.VMEM((tokens, width), F32)],
        compiler_params=pltpu.CompilerParams(vmem_limit_bytes=VMEM),
        cost_estimate=pl.CostEstimate(
            flops=2 * rows * tokens * width, bytes_accessed=10 * tokens * width, transcendentals=0
        ),
        name="first",
    )(attn, residual, gain, router, ids)


def others_kernel(base, attn_ref, res_ref, aux_ref, normed_ref, stream_ref, *packs):
    for g, pack_ref in enumerate(packs):
        pack_group(base, g + 1, aux_ref, normed_ref, pack_ref)
    width = res_ref.shape[1]
    quarter = width // STEPS
    for k in range(STEPS):
        cols = slice(k * quarter, (k + 1) * quarter)
        stream_ref[:, cols] = res_ref[:, cols].astype(F32) + attn_ref[cols, :].astype(F32).T


def others(base, attn, residual, aux, normed, rows):
    tokens, width = residual.shape
    return pl.pallas_call(
        functools.partial(others_kernel, base),
        out_shape=[jax.ShapeDtypeStruct((tokens, width), F32)]
        + [jax.ShapeDtypeStruct((rows, width // fold), BF16) for fold in FOLDS[1:]],
        compiler_params=pltpu.CompilerParams(vmem_limit_bytes=VMEM),
        cost_estimate=pl.CostEstimate(
            flops=4 * rows * tokens * width, bytes_accessed=14 * tokens * width, transcendentals=0
        ),
        name="others",
    )(attn, residual, aux, normed)


def inward_kernel(base, fold, parts, *refs):
    piece_refs = refs[:parts]
    gate_ref, up_ref, out_ref, acc = refs[parts:]
    few = base // fold
    ff = gate_ref.shape[2]
    step = pl.program_id(0)

    @pl.when(step == 0)
    def _():
        acc[...] = jnp.zeros_like(acc)

    pieces = [ref[...] for ref in piece_refs]
    if fold > 1:
        part = step // (STEPS // fold)
        rows = pieces[0].shape[0]
        out_row = lax.broadcasted_iota(jnp.int32, (rows // fold, rows), 0)
        in_row = lax.broadcasted_iota(jnp.int32, (rows // fold, rows), 1)
        select = as_mask(in_row == (out_row // few) * base + part * few + out_row % few)
        pieces = [dot(select, piece).astype(BF16) for piece in pieces]
    block = jnp.concatenate(pieces, axis=0)
    acc[:, :ff] += dot(block, gate_ref[0])
    acc[:, ff:] += dot(block, up_ref[0])

    @pl.when(step == STEPS - 1)
    def _():
        gated = acc[:, :ff]
        out_ref[...] = (gated / (1.0 + jnp.exp(-gated)) * acc[:, ff:]).astype(BF16)


def inward(base, fold, pieces, gate, up):
    width, ff = gate.shape[1:]
    quarter = width // STEPS
    total = sum(piece.shape[0] for piece in pieces) // fold
    return pl.pallas_call(
        functools.partial(inward_kernel, base, fold, len(pieces)),
        grid=(STEPS,),
        in_specs=[
            pl.BlockSpec((piece.shape[0], quarter), lambda i: (0, i % (STEPS // fold)))
            for piece in pieces
        ]
        + [pl.BlockSpec((1, quarter, ff), lambda i: (0, i, 0))] * 2,
        out_specs=pl.BlockSpec((total, ff), lambda i: (0, 0)),
        out_shape=jax.ShapeDtypeStruct((total, ff), BF16),
        scratch_shapes=[pltpu.VMEM((total, 2 * ff), F32)],
        compiler_params=pltpu.CompilerParams(vmem_limit_bytes=VMEM),
        cost_estimate=pl.CostEstimate(flops=total, bytes_accessed=total, transcendentals=0),
        name="inward",
    )(*pieces, gate, up)


def outward_kernel(base, fold, parts, here_ref, *refs):
    hidden, (down_ref, out_ref), scratch = refs[:parts], refs[parts : parts + 2], refs[parts + 2 :]
    here = here_ref[0]
    rows = out_ref.shape[1]
    few = base // fold
    count = rows // base * few
    ff = hidden[0].shape[1]
    made = None
    for o in range(parts):
        order = [(j - o) % parts for j in range(parts)]
        block = jnp.concatenate([hidden[o][i * count : (i + 1) * count, :] for i in order], axis=0)
        at = pl.multiple_of(lax.rem(here + parts - o, parts) * ff, ff)
        term = dot_nt(block, down_ref[0, :, pl.ds(at, ff)])
        made = term if made is None else made + term
    made = made.astype(BF16)
    pieces = [made[j * count : (j + 1) * count] for j in range(parts)]
    owners = [lax.rem(here + parts - j, parts) for j in range(parts)]
    if fold == 1:
        for owner, piece in zip(owners, pieces):
            out_ref[owner] = piece
        return
    (folded,) = scratch
    part, last = pl.program_id(1), pl.num_programs(1) - 1
    out_row = lax.broadcasted_iota(jnp.int32, (rows, count), 0)
    in_row = lax.broadcasted_iota(jnp.int32, (rows, count), 1)
    place = as_mask(out_row == (in_row // few) * base + part * few + in_row % few)

    @pl.when(part == 0)
    def _():
        folded[...] = jnp.zeros_like(folded)

    for j in range(parts):
        folded[j] += dot(place, pieces[j])

    @pl.when(part == last)
    def _():
        for j in range(parts):
            out_ref[owners[j]] = folded[j].astype(BF16)


def outward(base, fold, back_fold, here, hidden, down):
    parts = len(hidden)
    total, ff = hidden[0].shape
    rows = total // parts * fold
    cols = down.shape[1]
    steps = max(s for s in (1, 2, STEPS) if cols % (128 * s) == 0)
    step = cols // steps
    outer = steps // back_fold
    return pl.pallas_call(
        functools.partial(outward_kernel, base, fold, parts),
        grid_spec=pltpu.PrefetchScalarGridSpec(
            num_scalar_prefetch=1,
            grid=(outer, back_fold),
            in_specs=[pl.BlockSpec((total, ff), lambda i, h, here: (0, 0))] * parts
            + [pl.BlockSpec((1, step, parts * ff), lambda i, h, here: (0, h * outer + i, 0))],
            out_specs=pl.BlockSpec((parts, rows, step), lambda i, h, here: (0, 0, i)),
            scratch_shapes=[pltpu.VMEM((parts, rows, step), F32)] if fold > 1 else [],
        ),
        out_shape=jax.ShapeDtypeStruct((parts, rows, cols // back_fold), BF16),
        compiler_params=pltpu.CompilerParams(vmem_limit_bytes=VMEM),
        cost_estimate=pl.CostEstimate(flops=total, bytes_accessed=total, transcendentals=0),
        name="outward",
    )(here, *hidden, down)


def combine_kernel(base, fold, back_fold, group, aux_ref, stream_ref, back_ref, out_ref):
    rows, cols = back_ref.shape[1:]
    for h in range(back_fold):
        hits = placed(aux_ref, group, rows, h * (base // fold))
        both = sum(jnp.where(hits[k], aux_ref[k : k + 1, :], 0.0) for k in range(2)).T
        high = both.astype(BF16)
        low = (both - high.astype(F32)).astype(BF16)
        block = back_ref[0]
        cut = slice(h * cols, (h + 1) * cols)
        total = stream_ref[:, cut] + (dot(low, block) + dot(high, block))
        out_ref[:, cut] = total.astype(out_ref.dtype)


def combine(base, fold, back_fold, group, aux, stream, back):
    parts, rows, wide = back.shape
    tokens, width = stream.shape
    cols = width // parts
    last = group == len(FOLDS) - 1
    return pl.pallas_call(
        functools.partial(combine_kernel, base, fold, back_fold, group),
        grid=(parts,),
        in_specs=[
            pl.BlockSpec(aux.shape, lambda i: (0, 0)),
            pl.BlockSpec((tokens, cols), lambda i: (0, i)),
            pl.BlockSpec((1, rows, wide), lambda i: (i, 0, 0)),
        ],
        out_specs=pl.BlockSpec((tokens, cols), lambda i: (0, i)),
        out_shape=jax.ShapeDtypeStruct((tokens, width), BF16 if last else F32),
        compiler_params=pltpu.CompilerParams(vmem_limit_bytes=VMEM),
        cost_estimate=pl.CostEstimate(
            flops=4 * tokens * rows * width,
            bytes_accessed=8 * tokens * width + 2 * rows * wide * parts,
            transcendentals=0,
        ),
        name="combine",
    )(aux, stream, back)


def body(
    attn_cols, residual, norm_gain, router_weight, expert_ids, gate_weight, up_weight, down_weight
):
    groups = lax.axis_size("dp")
    parts = lax.axis_size("blk")
    tokens, width = residual.shape
    experts = router_weight.shape[1]
    fanout = expert_ids.shape[1]
    assert gate_weight.shape[0] == 1 and fanout == 2
    capacity = max(2, (5 * tokens * fanout + 4 * experts - 1) // (4 * experts))
    base = capacity * 2 // 5
    assert sum(base // fold for fold in FOLDS) == capacity
    rows = experts * base
    cols = down_weight.shape[1]
    here = lax.axis_index("blk").astype(jnp.int32).reshape(1)

    def shared(block):
        shifts = [[(i, (i + o) % parts) for i in range(parts)] for o in range(1, parts)]
        return [block] + [lax.ppermute(block, "blk", perm) for perm in shifts]

    def dispatch(pack):
        pack = pack.reshape(groups, base, -1)
        got = lax.all_to_all(pack, "dp", split_axis=0, concat_axis=0, tiled=True)
        return got.reshape(rows, -1)

    held = attn_cols.shape[1]
    send = attn_cols.T.reshape(held, groups, tokens).transpose(1, 0, 2)
    attn = lax.all_to_all(send, "dp", split_axis=0, concat_axis=0, tiled=True)
    attn = attn.reshape(width, tokens)
    aux, normed, pack = first(
        base, attn, residual, norm_gain.reshape(1, width), router_weight.T, expert_ids.T
    )
    stream, *packs = others(base, attn, residual, aux, normed, rows)
    def returned(made):
        made = made.reshape(parts * groups, base, -1)
        back = lax.all_to_all(made, ("blk", "dp"), split_axis=0, concat_axis=0, tiled=True)
        return back.reshape(parts, rows, -1)

    def gate_up(group, pieces):
        return inward(base, FOLDS[group], pieces, gate_weight, up_weight)

    back_folds = [fold if cols % (128 * fold) == 0 else 1 for fold in FOLDS]

    def down(group, hidden):
        return outward(base, FOLDS[group], back_folds[group], here, hidden, down_weight)

    tie = lax.optimization_barrier
    arrived_a, arrived_b = dispatch(pack), dispatch(packs[0])
    pieces_a, pieces_b = shared(arrived_a), shared(arrived_b)
    pieces_a, pieces_b[0] = tie((pieces_a, pieces_b[0]))
    hidden = gate_up(0, pieces_a)
    hidden, pack_c = tie((hidden, packs[1]))
    arrived_c = dispatch(pack_c)
    made = down(0, shared(hidden))
    made, pieces_b, arrived_c = tie((made, pieces_b, arrived_c))
    back_a = returned(made)
    hidden = shared(gate_up(1, pieces_b))
    hidden, arrived_c = tie((hidden, arrived_c))
    pieces_c = shared(arrived_c)
    made = down(1, hidden)
    made, pieces_c = tie((made, pieces_c))
    back_b = returned(made)
    back_c = returned(down(2, shared(gate_up(2, pieces_c))))
    for group, back in enumerate((back_a, back_b, back_c)):
        stream = combine(base, FOLDS[group], back_folds[group], group, aux, stream, back)
    return stream


def solution(mesh):
    return jax.shard_map(
        body,
        mesh=mesh,
        in_specs=(
            P("blk", "dp"),
            P(("blk", "dp"), None),
            P(),
            P(),
            P(("blk", "dp"), None),
            P("dp", None, "blk"),
            P("dp", None, "blk"),
            P("dp", "blk", None),
        ),
        out_specs=P(("blk", "dp"), None),
        check_vma=False,
    )
```

```python
import functools

import jax
import jax.numpy as jnp
from jax import lax
from jax.experimental import pallas as pl
from jax.experimental.pallas import tpu as pltpu
from jax.sharding import PartitionSpec as P

FOLDS = (1, 1, 2)
STEPS = 4
VMEM = 58 * 1024 * 1024
F32 = jnp.float32
BF16 = jnp.bfloat16


def dot(a, b):
    return lax.dot_general(a, b, (((1,), (0,)), ((), ())), preferred_element_type=F32)


def dot_nt(a, b):
    return lax.dot_general(a, b, (((1,), (1,)), ((), ())), preferred_element_type=F32)


def as_mask(cond):
    return jnp.where(cond, 1.0, 0.0).astype(BF16)


def placed(aux_ref, group, rows, shift):
    row = lax.broadcasted_iota(jnp.int32, (rows, aux_ref.shape[1]), 0).astype(F32) - shift
    at = 2 + 2 * group
    return [row == aux_ref[at + k : at + k + 1, :] for k in range(2)]


def pack_group(base, group, aux_ref, normed, pack_ref):
    fold = FOLDS[group]
    cols = pack_ref.shape[1]
    block = min(cols, normed.shape[1] // STEPS)
    picks = []
    for h in range(fold):
        first, second = placed(aux_ref, group, pack_ref.shape[0], h * (base // fold))
        picks.append(as_mask(first | second))
    for c in range(0, cols, block):
        total = None
        for h in range(fold):
            term = dot(picks[h], normed[:, h * cols + c : h * cols + c + block])
            total = term if total is None else total + term
        pack_ref[:, c : c + block] = total.astype(BF16)


def first_kernel(base, attn_ref, res_ref, gain_ref, router_ref, ids_ref, aux_ref, normed_ref, pack_ref, held):
    tokens, width = res_ref.shape
    experts = router_ref.shape[0]
    quarter = width // STEPS
    total = jnp.zeros((tokens, 1), F32)
    for k in range(STEPS):
        cols = slice(k * quarter, (k + 1) * quarter)
        part = res_ref[:, cols].astype(F32) + attn_ref[cols, :].astype(F32).T
        held[:, cols] = part
        total += jnp.sum(part * part, axis=1, keepdims=True)
    scale = lax.rsqrt(total / width + 1e-06)
    logits = jnp.zeros((experts, tokens), F32)
    for k in range(STEPS):
        cols = slice(k * quarter, (k + 1) * quarter)
        piece = (held[:, cols] * scale * gain_ref[:, cols].astype(F32)).astype(BF16)
        normed_ref[:, cols] = piece
        logits += dot_nt(router_ref[:, cols], piece)
    affinity = jax.nn.sigmoid(logits)
    expert = lax.broadcasted_iota(jnp.int32, (experts, tokens), 0)
    hit = [expert == ids_ref[k : k + 1, :] for k in range(2)]
    named = as_mask(hit[0] | hit[1])
    first = lax.broadcasted_iota(jnp.int32, (tokens, tokens), 0)
    second = lax.broadcasted_iota(jnp.int32, (tokens, tokens), 1)
    before = dot(named, as_mask(first < second))
    chosen = [jnp.sum(jnp.where(h, affinity, 0.0), axis=0, keepdims=True) for h in hit]
    ranks = [
        jnp.sum(jnp.where(h, before, 0.0), axis=0, keepdims=True).astype(jnp.int32) for h in hit
    ]
    denom = chosen[0] + chosen[1]
    for k in range(2):
        aux_ref[k : k + 1, :] = 2.5 * chosen[k] / denom
        start = 0
        for g, fold in enumerate(FOLDS):
            slots = base // fold
            inside = (ranks[k] >= start) & (ranks[k] < start + slots)
            row = ids_ref[k : k + 1, :] * base + ranks[k] - start
            at = 2 + 2 * g + k
            aux_ref[at : at + 1, :] = jnp.where(inside, row, -experts * base).astype(F32)
            start += slots
    pack_group(base, 0, aux_ref, normed_ref, pack_ref)


def first(base, attn, residual, gain, router, ids):
    tokens, width = residual.shape
    rows = router.shape[0] * base
    return pl.pallas_call(
        functools.partial(first_kernel, base),
        out_shape=[
            jax.ShapeDtypeStruct((8, tokens), F32),
            jax.ShapeDtypeStruct((tokens, width), BF16),
            jax.ShapeDtypeStruct((rows, width // FOLDS[0]), BF16),
        ],
        scratch_shapes=[pltpu.VMEM((tokens, width), F32)],
        compiler_params=pltpu.CompilerParams(vmem_limit_bytes=VMEM),
        cost_estimate=pl.CostEstimate(
            flops=2 * rows * tokens * width, bytes_accessed=10 * tokens * width, transcendentals=0
        ),
        name="first",
    )(attn, residual, gain, router, ids)


def others_kernel(base, attn_ref, res_ref, aux_ref, normed_ref, stream_ref, *packs):
    for g, pack_ref in enumerate(packs):
        pack_group(base, g + 1, aux_ref, normed_ref, pack_ref)
    width = res_ref.shape[1]
    quarter = width // STEPS
    for k in range(STEPS):
        cols = slice(k * quarter, (k + 1) * quarter)
        stream_ref[:, cols] = res_ref[:, cols].astype(F32) + attn_ref[cols, :].astype(F32).T


def others(base, attn, residual, aux, normed, rows):
    tokens, width = residual.shape
    return pl.pallas_call(
        functools.partial(others_kernel, base),
        out_shape=[jax.ShapeDtypeStruct((tokens, width), F32)]
        + [jax.ShapeDtypeStruct((rows, width // fold), BF16) for fold in FOLDS[1:]],
        compiler_params=pltpu.CompilerParams(vmem_limit_bytes=VMEM),
        cost_estimate=pl.CostEstimate(
            flops=4 * rows * tokens * width, bytes_accessed=14 * tokens * width, transcendentals=0
        ),
        name="others",
    )(attn, residual, aux, normed)


def inward_kernel(base, fold, parts, *refs):
    piece_refs = refs[:parts]
    gate_ref, up_ref, out_ref, acc = refs[parts:]
    few = base // fold
    ff = gate_ref.shape[2]
    step = pl.program_id(0)

    @pl.when(step == 0)
    def _():
        acc[...] = jnp.zeros_like(acc)

    pieces = [ref[...] for ref in piece_refs]
    if fold > 1:
        part = step // (STEPS // fold)
        unfolded = []
        for piece in pieces:
            rows = piece.shape[0]
            out_row = lax.broadcasted_iota(jnp.int32, (rows // fold, rows), 0)
            in_row = lax.broadcasted_iota(jnp.int32, (rows // fold, rows), 1)
            select = as_mask(in_row == (out_row // few) * base + part * few + out_row % few)
            unfolded.append(dot(select, piece).astype(BF16))
        pieces = unfolded
    block = jnp.concatenate(pieces, axis=0)
    acc[:, :ff] += dot(block, gate_ref[0])
    acc[:, ff:] += dot(block, up_ref[0])

    @pl.when(step == STEPS - 1)
    def _():
        gated = acc[:, :ff]
        out_ref[...] = (gated / (1.0 + jnp.exp(-gated)) * acc[:, ff:]).astype(BF16)


def inward(base, fold, pieces, gate, up):
    width, ff = gate.shape[1:]
    quarter = width // STEPS
    total = sum(piece.shape[0] for piece in pieces) // fold
    return pl.pallas_call(
        functools.partial(inward_kernel, base, fold, len(pieces)),
        grid=(STEPS,),
        in_specs=[
            pl.BlockSpec((piece.shape[0], quarter), lambda i: (0, i % (STEPS // fold)))
            for piece in pieces
        ]
        + [pl.BlockSpec((1, quarter, ff), lambda i: (0, i, 0))] * 2,
        out_specs=pl.BlockSpec((total, ff), lambda i: (0, 0)),
        out_shape=jax.ShapeDtypeStruct((total, ff), BF16),
        scratch_shapes=[pltpu.VMEM((total, 2 * ff), F32)],
        compiler_params=pltpu.CompilerParams(vmem_limit_bytes=VMEM),
        cost_estimate=pl.CostEstimate(flops=total, bytes_accessed=total, transcendentals=0),
        name="inward",
    )(*pieces, gate, up)


def outward_kernel(base, fold, parts, here_ref, *refs):
    hidden, (down_ref, out_ref), scratch = refs[:parts], refs[parts : parts + 2], refs[parts + 2 :]
    here = here_ref[0]
    rows = out_ref.shape[1]
    few = base // fold
    count = rows // base * few
    ff = hidden[0].shape[1]
    made = None
    for o in range(parts):
        order = [(j - o) % parts for j in range(parts)]
        block = jnp.concatenate([hidden[o][i * count : (i + 1) * count, :] for i in order], axis=0)
        at = pl.multiple_of(lax.rem(here + parts - o, parts) * ff, ff)
        term = dot_nt(block, down_ref[0, :, pl.ds(at, ff)])
        made = term if made is None else made + term
    made = made.astype(BF16)
    pieces = [made[j * count : (j + 1) * count] for j in range(parts)]
    owners = [lax.rem(here + parts - j, parts) for j in range(parts)]
    if fold == 1:
        for owner, piece in zip(owners, pieces):
            out_ref[owner] = piece
        return
    (folded,) = scratch
    part, last = pl.program_id(1), pl.num_programs(1) - 1
    out_row = lax.broadcasted_iota(jnp.int32, (rows, count), 0)
    in_row = lax.broadcasted_iota(jnp.int32, (rows, count), 1)
    place = as_mask(out_row == (in_row // few) * base + part * few + in_row % few)

    @pl.when(part == 0)
    def _():
        folded[...] = jnp.zeros_like(folded)

    for j in range(parts):
        folded[j] += dot(place, pieces[j])

    @pl.when(part == last)
    def _():
        for j in range(parts):
            out_ref[owners[j]] = folded[j].astype(BF16)


def outward(base, fold, back_fold, here, hidden, down):
    parts = len(hidden)
    total, ff = hidden[0].shape
    rows = total // parts * fold
    cols = down.shape[1]
    steps = max(s for s in (1, 2, STEPS) if cols % (128 * s) == 0)
    step = cols // steps
    outer = steps // back_fold
    return pl.pallas_call(
        functools.partial(outward_kernel, base, fold, parts),
        grid_spec=pltpu.PrefetchScalarGridSpec(
            num_scalar_prefetch=1,
            grid=(outer, back_fold),
            in_specs=[pl.BlockSpec((total, ff), lambda i, h, here: (0, 0))] * parts
            + [pl.BlockSpec((1, step, parts * ff), lambda i, h, here: (0, h * outer + i, 0))],
            out_specs=pl.BlockSpec((parts, rows, step), lambda i, h, here: (0, 0, i)),
            scratch_shapes=[pltpu.VMEM((parts, rows, step), F32)] if fold > 1 else [],
        ),
        out_shape=jax.ShapeDtypeStruct((parts, rows, cols // back_fold), BF16),
        compiler_params=pltpu.CompilerParams(vmem_limit_bytes=VMEM),
        cost_estimate=pl.CostEstimate(flops=total, bytes_accessed=total, transcendentals=0),
        name="outward",
    )(here, *hidden, down)


def combine_kernel(base, fold, back_fold, group, aux_ref, stream_ref, back_ref, out_ref):
    rows, cols = back_ref.shape[1:]
    for h in range(back_fold):
        hits = placed(aux_ref, group, rows, h * (base // fold))
        both = sum(jnp.where(hits[k], aux_ref[k : k + 1, :], 0.0) for k in range(2)).T
        high = both.astype(BF16)
        low = (both - high.astype(F32)).astype(BF16)
        block = back_ref[0]
        cut = slice(h * cols, (h + 1) * cols)
        total = stream_ref[:, cut] + (dot(low, block) + dot(high, block))
        out_ref[:, cut] = total.astype(out_ref.dtype)


def combine(base, fold, back_fold, group, aux, stream, back):
    parts, rows, wide = back.shape
    tokens, width = stream.shape
    cols = width // parts
    last = group == len(FOLDS) - 1
    return pl.pallas_call(
        functools.partial(combine_kernel, base, fold, back_fold, group),
        grid=(parts,),
        in_specs=[
            pl.BlockSpec(aux.shape, lambda i: (0, 0)),
            pl.BlockSpec((tokens, cols), lambda i: (0, i)),
            pl.BlockSpec((1, rows, wide), lambda i: (i, 0, 0)),
        ],
        out_specs=pl.BlockSpec((tokens, cols), lambda i: (0, i)),
        out_shape=jax.ShapeDtypeStruct((tokens, width), BF16 if last else F32),
        compiler_params=pltpu.CompilerParams(vmem_limit_bytes=VMEM),
        cost_estimate=pl.CostEstimate(
            flops=4 * tokens * rows * width,
            bytes_accessed=8 * tokens * width + 2 * rows * wide * parts,
            transcendentals=0,
        ),
        name="combine",
    )(aux, stream, back)


def body(
    attn_cols, residual, norm_gain, router_weight, expert_ids, gate_weight, up_weight, down_weight
):
    groups = lax.axis_size("dp")
    parts = lax.axis_size("blk")
    tokens, width = residual.shape
    experts = router_weight.shape[1]
    fanout = expert_ids.shape[1]
    assert gate_weight.shape[0] == 1 and fanout == 2
    capacity = max(2, (5 * tokens * fanout + 4 * experts - 1) // (4 * experts))
    base = capacity * 2 // 5
    assert sum(base // fold for fold in FOLDS) == capacity
    rows = experts * base
    cols = down_weight.shape[1]
    here = lax.axis_index("blk").astype(jnp.int32).reshape(1)

    def shared(block, cuts=1):
        shifts = [[(i, (i + o) % parts) for i in range(parts)] for o in range(1, parts)]
        sent = jnp.split(block, cuts, axis=0)
        return [block] + [lax.ppermute(piece, "blk", perm) for perm in shifts for piece in sent]

    def dispatch(pack):
        pack = pack.reshape(groups, base, -1)
        got = lax.all_to_all(pack, "dp", split_axis=0, concat_axis=0, tiled=True)
        return got.reshape(rows, -1)

    held = attn_cols.shape[1]
    send = attn_cols.T.reshape(held, groups, tokens).transpose(1, 0, 2)
    attn = lax.all_to_all(send, "dp", split_axis=0, concat_axis=0, tiled=True)
    attn = attn.reshape(width, tokens)
    aux, normed, pack = first(
        base, attn, residual, norm_gain.reshape(1, width), router_weight.T, expert_ids.T
    )
    stream, *packs = others(base, attn, residual, aux, normed, rows)
    def returned(made):
        made = made.reshape(parts * groups, base, -1)
        back = lax.all_to_all(made, ("blk", "dp"), split_axis=0, concat_axis=0, tiled=True)
        return back.reshape(parts, rows, -1)

    def gate_up(group, pieces):
        return inward(base, FOLDS[group], pieces, gate_weight, up_weight)

    back_folds = [fold if cols % (128 * fold) == 0 else 1 for fold in FOLDS]

    def down(group, hidden):
        return outward(base, FOLDS[group], back_folds[group], here, hidden, down_weight)

    tie = lax.optimization_barrier
    arrived_a, arrived_b = dispatch(pack), dispatch(packs[0])
    pieces_a, pieces_b = shared(arrived_a), shared(arrived_b)
    pieces_a, pieces_b[0] = tie((pieces_a, pieces_b[0]))
    hidden = gate_up(0, pieces_a)
    hidden, pack_c = tie((hidden, packs[1]))
    arrived_c = dispatch(pack_c)
    made = down(0, shared(hidden))
    made, pieces_b, arrived_c = tie((made, pieces_b, arrived_c))
    back_a = returned(made)
    hidden = shared(gate_up(1, pieces_b))
    hidden, arrived_c = tie((hidden, arrived_c))
    pieces_c = shared(arrived_c, 2)
    made = down(1, hidden)
    made, pieces_c[1::2] = tie((made, pieces_c[1::2]))
    back_b = returned(made)
    back_c = returned(down(2, shared(gate_up(2, pieces_c))))
    for group, back in enumerate((back_a, back_b, back_c)):
        stream = combine(base, FOLDS[group], back_folds[group], group, aux, stream, back)
    return stream


def solution(mesh):
    return jax.shard_map(
        body,
        mesh=mesh,
        in_specs=(
            P("blk", "dp"),
            P(("blk", "dp"), None),
            P(),
            P(),
            P(("blk", "dp"), None),
            P("dp", None, "blk"),
            P("dp", None, "blk"),
            P("dp", "blk", None),
        ),
        out_specs=P(("blk", "dp"), None),
        check_vma=False,
    )
```
